32 devices in a mesh: parts: 2 (over y), bank: 4 (over z), tm: 2 (over x), rate: 2 (over core).
Axes of the slice: x: 2, y: 2, z: 4, core: 2. Of those that a mesh axis runs over, the one named last changes fastest.
Arguments:
- strain: float32 [2, 16384], P('rate', ('parts', 'bank', 'tm')), parts along dimension 1, may hold values from -6 to 6
- gate_mask: int32 [16384], P(('parts', 'bank', 'tm')), parts along dimension 0, may hold values 0 or 1
- psd_reset: int32 [16], P(('parts', 'bank', 'tm')), parts along dimension 0, may hold values from 0 to 1
- psd_ref: float32 [2, 512], P('rate'), may hold values from 0.1 to 10
- psd_rate: float32 [2, 512], P('rate'), may hold values from 0.025 to 0.5
- filters: bfloat16 [4, 2, 32, 2048], P('bank', 'rate'), may hold values from -0.125 to 0.125
- basis_count: int32 [4], P('bank'), may hold values from 16 to 32, as said below
- mixing: bfloat16 [4, 2, 4, 2, 32], P('bank', 'rate'), may hold values from -0.75 to 0.75
- autocorrelation: float32 [4, 2, 257], replicated, may hold values from -1.2 to 1.2
Outputs:
- snr_sq: float32 [4, 4, 16384], P(None, 'rate', ('parts', 'bank', 'tm')), parts along dimension 2
- chisq: float32 [4, 4, 16384], P(None, 'rate', ('parts', 'bank', 'tm')), parts along dimension 2
The draws below stay inside these ranges and needn't reach their ends.
There are 2 independent parts, one for each index of `parts`. The reference program is written for one: setup_inputs(seed, part) draws one part's arguments, and reference() takes and returns one part's arrays. A program takes and returns all parts, laid end to end along the dimension named above; an argument that names none is the same for every part. Nothing has to cross between parts.
Inputs may be any that keep to these rules, and one draw needn't show every extreme that they name: `basis_count`: some bank uses all 32 basis filters and another only half of them.
All inputs are finite; a program needn't handle non-finite values. No bound on the sum of `gate_mask` on one device may be relied on, other than what follows from the above.
Results may differ from the reference program's by a relative error of at most 0.0044.
Values may be sent and summed in bfloat16 or wider, within the bound.
A program may use at most 128 MiB of HBM per device.

```python
import math
import jax
import jax.numpy as jnp
from jax import lax

PIECE = 1024
TAPS = 2048
BASIS = 32
TEMPL = 4
ACL_HALF = 128
BANKS = 4
BANDS = 2
PIECES = 8
TIME = 8192
BINS = 512
ACL = 257


def draw_basis_count(key, part):
    key_one = jax.random.fold_in(key, 11)
    key_two = jax.random.fold_in(key, 12)
    key_three = jax.random.fold_in(key, 13)
    counts = jax.random.randint(key_one, (BANKS,), BASIS // 2, BASIS + 1)
    top_bank = jax.random.randint(key_two, (), 0, BANKS)
    low_bank = (top_bank + 1 + jax.random.randint(key_three, (), 0, BANKS - 1)) % BANKS
    positions = jnp.arange(BANKS)
    counts = jnp.where(positions == top_bank, BASIS, counts)
    counts = jnp.where(positions == low_bank, BASIS // 2, counts)
    return counts.astype(jnp.int32)


def draw_psd_reset(key, part):
    key_one = jax.random.fold_in(key, 21)
    rolls = jax.random.randint(key_one, (PIECES,), 0, 8)
    resets = jnp.where(rolls == 0, 1, 0)
    positions = jnp.arange(PIECES)
    first_block = part % PIECES
    second_block = (part + 1) % PIECES
    resets = jnp.where(positions == first_block, 1, resets)
    resets = jnp.where(positions == second_block, 0, resets)
    return resets.astype(jnp.int32)


def touch_ends(values, stream_key, low, top_value):
    spot = [jax.random.randint(jax.random.fold_in(stream_key, axis), (), 0, length) for axis, length in enumerate(values.shape)]
    widest = values.shape.index(max(values.shape))
    next_to = spot[:widest] + [(spot[widest] + 1) % values.shape[widest]] + spot[widest + 1:]
    return values.at[tuple(spot)].set(low).at[tuple(next_to)].set(top_value)


def block_levels(rng, extent, pieces, least, high):
    loudness, own = 1.0, jax.random.fold_in(rng, 6)
    for dim, parts in pieces:
        draws = jnp.exp(jax.random.uniform(jax.random.fold_in(own, dim), (parts,), jnp.float32, least / len(pieces), high / len(pieces)))
        loudness = loudness * jnp.repeat(draws, extent[dim] // parts).reshape([-1 if axis == dim else 1 for axis in range(len(extent))])
    return loudness


def normal_values(stream_key, extent, deviation, reach, split=(), kind=jnp.bfloat16):
    result = jax.random.normal(stream_key, extent, jnp.float32) * deviation
    if len(split) > 0:
        result = block_levels(stream_key, extent, split, -0.22, 0.18) * result
    return jnp.clip(result, min=-reach, max=reach).astype(kind)


def setup_inputs(seed: int = 0, part: int = 0) -> dict:
    splits = jax.random.split(jax.random.key(seed), 10)
    part_splits = jax.random.split(jax.random.fold_in(splits[9], part), 10)
    return {
        "strain": normal_values(part_splits[0], (BANDS, TIME), 1.0, 6.0, ((0, 2), (1, 8)), jnp.float32),
        "gate_mask": touch_ends((jax.random.randint(part_splits[1], (TIME,), 0, 32) < 31).astype(jnp.int32), jax.random.fold_in(part_splits[1], 1), 0, 1),
        "psd_reset": draw_psd_reset(jax.random.fold_in(jax.random.fold_in(splits[9], part), 71), part),
        "psd_ref": jnp.clip(jnp.exp(math.log(10.0) - 4.6051702 * jax.random.uniform(splits[3], (BANDS, BINS), jnp.float32) ** block_levels(splits[3], (BANDS, BINS), ((0, 2),), -0.2, 0.2)), 0.1, 10.0),
        "psd_rate": jnp.clip(jnp.exp(math.log(0.5) - 2.9957323 * jax.random.uniform(splits[4], (BANDS, BINS), jnp.float32) ** block_levels(splits[4], (BANDS, BINS), ((0, 2),), -0.2, 0.2)), 0.025, 0.5),
        "filters": normal_values(splits[5], (BANKS, BANDS, BASIS, TAPS), TAPS ** -0.5, 0.125, ((0, 4), (1, 2))),
        "basis_count": draw_basis_count(jax.random.fold_in(splits[9], 71), part),
        "mixing": normal_values(splits[7], (BANKS, BANDS, TEMPL, 2, BASIS), (2 * BASIS) ** -0.5, 0.75, ((0, 4), (1, 2))),
        "autocorrelation": normal_values(splits[8], (BANKS, 2, ACL), 0.3, 1.2, (), jnp.float32),
    }


HIGHEST = lax.Precision.HIGHEST


def dft_tables(length):
    bin_count = length // 2
    sample = jnp.arange(length, dtype=jnp.int32)
    frequency = jnp.arange(bin_count, dtype=jnp.int32)
    phase_index = (sample[:, None] * frequency[None, :]) % length
    angle_value = phase_index.astype(jnp.float32) * (2.0 * math.pi / length)
    weights = jnp.where(frequency == 0, 1.0 / length, 2.0 / length).astype(jnp.float32)
    return jnp.cos(angle_value), jnp.sin(angle_value), weights


def reference(strain, gate_mask, psd_reset, psd_ref, psd_rate, filters, basis_count, mixing, autocorrelation):
    cos_table, sin_table, weights = dft_tables(PIECE)
    gated = strain * gate_mask.astype(jnp.float32)[None, :]
    blocks = gated.reshape(BANDS, PIECES, PIECE)
    real_part = jnp.einsum('cgn,nk->cgk', blocks, cos_table, precision=HIGHEST)
    imag_part = jnp.einsum('cgn,nk->cgk', blocks, sin_table, precision=HIGHEST)
    log_power = jnp.log((real_part * real_part + imag_part * imag_part) / (PIECE / 2) + 0.1 * psd_ref[:, None, :])
    keep_factor = (1.0 - psd_rate)[:, None, :] * (1.0 - 0.5 * psd_reset.astype(jnp.float32))[None, :, None]
    drive_term = psd_rate[:, None, :] * log_power

    def advance(state_now, inputs):
        keep_now, drive_now = inputs
        state_next = keep_now * state_now + drive_now
        return state_next, state_next

    final_state, log_psd = lax.scan(advance, jnp.log(psd_ref), (keep_factor.transpose(1, 0, 2), drive_term.transpose(1, 0, 2)))
    log_psd = log_psd.transpose(1, 0, 2)
    bin_scale = jnp.exp(-0.5 * log_psd) * weights
    whitened = jnp.einsum('cgk,nk->cgn', real_part * bin_scale, cos_table, precision=HIGHEST)
    whitened = whitened + jnp.einsum('cgk,nk->cgn', imag_part * bin_scale, sin_table, precision=HIGHEST)
    whitened = whitened.reshape(BANDS, TIME).astype(jnp.bfloat16)

    fft_length = 2 ** int(math.ceil(math.log2(TIME + TAPS + 2 * ACL_HALF + 1)))
    spec_strain = jnp.fft.rfft(whitened.astype(jnp.float32), fft_length)
    ones_kernel = jnp.ones((ACL,), jnp.float32)
    ones_spec = jnp.fft.rfft(ones_kernel, fft_length)

    def per_bank(inputs):
        taps_bank, count_bank, mixing_bank, series_bank = inputs
        spec_taps = jnp.fft.rfft(taps_bank.astype(jnp.float32), fft_length)
        outputs = jnp.fft.irfft(spec_taps * spec_strain[:, None, :], fft_length)[..., :TIME]
        live_basis = (jnp.arange(BASIS, dtype=jnp.int32) < count_bank).astype(jnp.float32)
        basis = (outputs * live_basis[None, :, None]).astype(jnp.bfloat16)
        snr = jnp.einsum('cmpi,cit->mpt', mixing_bank.astype(jnp.float32), basis.astype(jnp.float32))
        energy = snr[:, 0] * snr[:, 0] + snr[:, 1] * snr[:, 1]
        complex_snr = snr[:, 0] + 1j * snr[:, 1]
        kernel = jnp.conj(series_bank[0] + 1j * series_bank[1])[::-1]
        folded = jnp.fft.ifft(jnp.fft.fft(complex_snr, fft_length) * jnp.fft.fft(kernel, fft_length))
        folded = folded[:, ACL_HALF:ACL_HALF + TIME]
        window_sum = jnp.fft.irfft(jnp.fft.rfft(energy, fft_length) * ones_spec, fft_length)[:, ACL_HALF:ACL_HALF + TIME]
        lag_energy = jnp.sum(series_bank * series_bank)
        cross = snr[:, 0] * jnp.real(folded) + snr[:, 1] * jnp.imag(folded)
        chisq = (window_sum - 2.0 * cross + energy * lag_energy) / ACL
        return energy, chisq

    snr_sq, chisq = lax.map(per_bank, (filters, basis_count, mixing, autocorrelation))
    return snr_sq, chisq
```

```python
import functools
import math

import jax
import jax.numpy as jnp
import numpy as np
from jax import lax
from jax.experimental import pallas as pl
from jax.experimental.pallas import tpu as pltpu
from jax.sharding import PartitionSpec as P

HIGHEST = lax.Precision.HIGHEST
F32 = jnp.float32
BF16 = jnp.bfloat16
LANES = 128
MESH = pl.DeviceIdType.MESH


def dft_constants(length, group):
    rows = length // LANES
    half = length // 2 // rows
    n1 = np.arange(rows)
    n2 = np.arange(LANES)
    small = 2.0 * np.pi * ((n1[:, None] * n1[None, :]) % rows) / rows
    eye = np.eye(group)
    first = np.concatenate([np.kron(eye, np.cos(small)), np.kron(eye, np.sin(small))], axis=0)
    last = np.concatenate([np.kron(eye, np.cos(small)), np.kron(eye, np.sin(small))], axis=1)
    angle = 2.0 * np.pi * (n1[:, None] * n2[None, :]) / length
    twiddle = np.stack([np.cos(angle), np.sin(angle)])
    wide = 2.0 * np.pi * ((n2[:, None] * n2[None, :]) % LANES) / LANES
    live = (n2 < half).astype(np.float64)
    c, s = np.cos(wide) * live, np.sin(wide) * live
    forward = np.concatenate(
        [np.concatenate([c, s], axis=1), np.concatenate([-s, c], axis=1)], axis=0
    )
    ct, st = c.T, s.T
    inverse = np.concatenate(
        [np.concatenate([ct, -st], axis=1), np.concatenate([st, ct], axis=1)], axis=0
    )
    return tuple(a.astype(np.float32) for a in (first, twiddle, forward, inverse, last))


def iota(shape, dim):
    return lax.broadcasted_iota(jnp.int32, shape, dim)


def each(count, step):
    if count <= 32:
        for i in range(count):
            step(i)
    else:
        lax.fori_loop(0, count, lambda i, c: (step(i), c)[1], 0)


def split(x):
    high = x.astype(BF16)
    return high, (x - high.astype(F32)).astype(BF16)


def nt_dot(a, b):
    return lax.dot_general(a, b, (((1,), (1,)), ((), ())), preferred_element_type=F32)


def kernel(
    sizes,
    strain,
    gate,
    reset,
    ref,
    rate,
    filters,
    count,
    mixing,
    auto,
    first,
    twiddle,
    forward,
    inverse,
    last,
    out_sq,
    out_chi,
    xbuf,
    pbuf,
    gsend,
    gbuf,
    wbuf,
    lbuf,
    yre,
    yim,
    rpad,
    rhi,
    rlo,
    x_send,
    x_recv,
    p_send,
    p_recv,
    g_send,
    g_recv,
):
    nb, ntm, nr, group = sizes
    nblk = nb * ntm
    slots = nr * nblk
    rows = xbuf.shape[1] // 2
    taps = filters.shape[1]
    lags = taps // LANES
    bank, tm, core = lax.axis_index("bank"), lax.axis_index("tm"), lax.axis_index("rate")
    block = bank * ntm + tm
    me = core * nblk + block

    def device(slot):
        blk = lax.rem(slot, nblk)
        return {"bank": blk // ntm, "tm": lax.rem(blk, ntm), "rate": slot // nblk}

    barrier = pltpu.get_barrier_semaphore()

    def greet(i):
        pl.semaphore_signal(
            barrier, inc=1, device_id=device(lax.rem(me + i + 1, slots)), device_id_type=MESH
        )

    each(slots - 1, greet)

    xbuf[me, 0:rows, :] = strain[...] * gate[...].astype(F32)
    xbuf[me, rows : 2 * rows, :] = jnp.full((rows, LANES), reset[0], jnp.int32).astype(F32)
    bin_rows = ref.shape[0]
    pbuf[core, 0:bin_rows, :] = ref[...]
    pbuf[core, bin_rows : 2 * bin_rows, :] = rate[...]

    pl.semaphore_wait(barrier, slots - 1)

    def x_copy(src_slot, target, i):
        return pltpu.make_async_remote_copy(
            src_ref=xbuf.at[src_slot],
            dst_ref=xbuf.at[src_slot],
            send_sem=x_send.at[i],
            recv_sem=x_recv.at[src_slot],
            device_id=device(target),
            device_id_type=MESH,
        )

    def p_copy(src_core, target, i):
        return pltpu.make_async_remote_copy(
            src_ref=pbuf.at[src_core],
            dst_ref=pbuf.at[src_core],
            send_sem=p_send.at[i],
            recv_sem=p_recv.at[src_core],
            device_id={"rate": target},
            device_id_type=MESH,
        )

    each(slots - 1, lambda i: x_copy(me, lax.rem(me + i + 1, slots), i).start())
    for i in range(nr - 1):
        p_copy(core, lax.rem(core + i + 1, nr), i).start()

    basis = filters.shape[0]
    mix_rows = mixing.shape[0]
    share = mix_rows // nr // 2
    live = (iota((mix_rows, basis), 1) < count[0]).astype(F32)
    dest, source = iota((mix_rows, mix_rows), 0), iota((mix_rows, mix_rows), 1)
    inner = dest % (2 * share)
    wanted = dest // (2 * share) * (2 * share) + inner % share * 2 + inner // share
    perm = (source == wanted).astype(F32)
    mixed_rows = jnp.dot(perm, mixing[...].astype(F32) * live, preferred_element_type=F32)
    mixed = jnp.dot(mixed_rows.astype(BF16), filters[...], preferred_element_type=F32)
    upper = iota((8, LANES), 0) < 4
    for r in range(nr):
        for quad in range(lags // 4):
            parts = []
            for h in range(2):
                at = (4 * quad + 2 * h) * LANES
                low, high = mixed[:, at : at + LANES], mixed[:, at + LANES : at + 2 * LANES]
                if r == 0:
                    high = pltpu.roll(high, 4, 0)
                else:
                    low = pltpu.roll(low, 4, 0)
                parts.append(jnp.where(upper, low, high))
            gsend[r, quad] = jnp.concatenate(parts, axis=0).astype(BF16)

    peers = nb * nr
    mine = core * nb + bank

    def g_copy(source, target, i):
        return pltpu.make_async_remote_copy(
            src_ref=gsend.at[target // nb],
            dst_ref=gbuf.at[source // nb, :, lax.rem(source, nb)],
            send_sem=g_send.at[i],
            recv_sem=g_recv.at[source],
            device_id={"bank": lax.rem(target, nb), "rate": target // nb},
            device_id_type=MESH,
        )

    each(peers - 1, lambda i: g_copy(mine, lax.rem(mine + i + 1, peers), i).start())
    gbuf[core, :, bank] = gsend[core]

    window = auto.shape[2] // 2
    span = 3 * LANES
    rpad[...] = jnp.zeros_like(rpad)
    for b in range(nb):
        for d in range(2):
            rpad[2 * b + d : 2 * b + d + 1, 0 : auto.shape[2]] = auto[b, d : d + 1, :]
    lag_energy = []
    for b in range(nb):
        series = rpad[2 * b : 2 * b + 2, :]
        lag_energy.append(jnp.sum(series * series, keepdims=True))

    def band(row):
        line = jnp.broadcast_to(rpad[pl.ds(row, 1), :], (LANES, span))
        high, low = split(pltpu.roll(line, 0, 1, stride=1, stride_axis=0))
        rhi[row] = high
        rlo[row] = low

    each(2 * nb, band)
    offset = iota((LANES, span), 1) - iota((LANES, span), 0)
    ones_band = ((offset >= 0) & (offset <= 2 * window)).astype(F32).astype(BF16)

    for i in range(nr - 1):
        p_copy(lax.rem(core + i + 1, nr), core, i).wait_recv()
    each(slots - 1, lambda i: x_copy(lax.rem(me + i + 1, slots), me, i).wait_recv())

    bins = bin_rows * LANES
    pick = iota((rows, LANES), 1) % rows == iota((rows, LANES), 0)
    lines = []
    for c in range(nr):
        for which in range(2):
            pieces = []
            for q in range(bin_rows):
                row = pbuf[c, which * bin_rows + q : which * bin_rows + q + 1, :]
                pieces.append(jnp.where(pick, jnp.broadcast_to(row, (rows, LANES)), 0.0))
            lines.append(jnp.concatenate(pieces, axis=1))
    gather = (iota((bins, LANES), 0) // rows == iota((bins, LANES), 1)).astype(F32)
    psd = jnp.dot(
        jnp.concatenate(lines, axis=0), gather, precision=HIGHEST, preferred_element_type=F32
    )
    lane = iota((rows, LANES), 1)
    live_bin = lane < bins // rows
    length = rows * LANES
    weight = jnp.where(
        live_bin,
        jnp.where((lane == 0) & (iota((rows, LANES), 0) == 0), 1.0 / length, 2.0 / length),
        0.0,
    )
    refs = [jnp.where(live_bin, psd[2 * c * rows : (2 * c + 1) * rows], 1.0) for c in range(nr)]
    rates = [psd[(2 * c + 1) * rows : (2 * c + 2) * rows] for c in range(nr)]

    tall = group * rows
    cos_tw = jnp.broadcast_to(twiddle[0][None], (group, rows, LANES)).reshape(tall, LANES)
    sin_tw = jnp.broadcast_to(twiddle[1][None], (group, rows, LANES)).reshape(tall, LANES)
    for s in range(slots // group):
        x = xbuf[s * group : (s + 1) * group, 0:rows, :].reshape(tall, LANES)
        y = jnp.dot(first[...], x, precision=HIGHEST, preferred_element_type=F32)
        a, b = y[:tall], y[tall:]
        turned = jnp.concatenate([a * cos_tw - b * sin_tw, a * sin_tw + b * cos_tw], axis=1)
        spec = jnp.dot(turned, forward[...], precision=HIGHEST, preferred_element_type=F32)
        real, imag = spec[:, :LANES], spec[:, LANES:]
        yre[s * group : (s + 1) * group] = real.reshape(group, rows, LANES)
        yim[s * group : (s + 1) * group] = imag.reshape(group, rows, LANES)
        power = (real * real + imag * imag) / (length / 2)
        lbuf[s * group : (s + 1) * group] = power.reshape(group, rows, LANES)

    def advance(i, states):
        after = []
        for c in range(nr):
            at = c * nblk + i
            keep = (1.0 - rates[c]) * (1.0 - 0.5 * xbuf[at, rows : 2 * rows, :])
            level = jnp.log(lbuf[at] + 0.1 * refs[c])
            state = keep * states[c] + rates[c] * level
            lbuf[at] = jnp.exp(-0.5 * state) * weight
            after.append(state)
        return tuple(after)

    states = tuple(jnp.log(refs[c]) for c in range(nr))
    if nblk <= 16:
        for i in range(nblk):
            states = advance(i, states)
    else:
        lax.fori_loop(0, nblk, advance, states)

    pad = wbuf.shape[1] - nblk * rows - rows
    for c in range(nr):
        wbuf[c, 0:pad, :] = jnp.zeros((pad, LANES), F32)
        wbuf[c, pad + nblk * rows :, :] = jnp.zeros((rows, LANES), F32)
    per_copy = min(group, nblk)
    for s in range(slots // group):
        scale = lbuf[s * group : (s + 1) * group].reshape(tall, LANES)
        real = yre[s * group : (s + 1) * group].reshape(tall, LANES) * scale
        imag = yim[s * group : (s + 1) * group].reshape(tall, LANES) * scale
        y = jnp.dot(
            jnp.concatenate([real, imag], axis=1),
            inverse[...],
            precision=HIGHEST,
            preferred_element_type=F32,
        )
        a, b = y[:, :LANES], y[:, LANES:]
        turned = jnp.concatenate([a * cos_tw + b * sin_tw, b * cos_tw - a * sin_tw], axis=0)
        white = jnp.dot(last[...], turned, precision=HIGHEST, preferred_element_type=F32)
        white = white.astype(BF16).astype(F32)
        for piece in range(group // per_copy):
            slot = s * group + piece * per_copy
            c, blk = slot // nblk, slot % nblk
            at = pad + blk * rows
            wbuf[c, at : at + per_copy * rows, :] = white[
                piece * per_copy * rows : (piece + 1) * per_copy * rows
            ]

    each(peers - 1, lambda i: g_copy(lax.rem(mine + i + 1, peers), mine, i).wait_recv())
    frames = rows + 2
    start = pl.multiple_of(block * rows, rows)
    view = [wbuf[c, pl.ds(start, pad + 2 * rows), :] for c in range(nr)]
    quads = lags // 4
    table = jnp.concatenate(
        [gbuf[c].reshape(quads * nb * 16, LANES) for c in range(nr)], axis=1
    )
    later = iota((LANES, LANES), 1) >= iota((LANES, LANES), 0)

    def spun(c, row):
        line = jnp.broadcast_to(view[c][row : row + 1, :], (LANES, LANES))
        return pltpu.roll(line, 0, 1, stride=1, stride_axis=0)

    total = [None] * (frames + 1)
    before = [spun(c, pad - lags - 1) for c in range(nr)]
    for a in range(frames + lags - 1):
        now = [spun(c, pad - lags + a) for c in range(nr)]
        toeplitz = jnp.concatenate(
            [jnp.where(later, now[c], before[c]).astype(BF16) for c in range(nr)], axis=0
        )
        before = now
        lowest = max(0, -((a - lags + 4) // 4))
        highest = min(quads - 1, (frames - 1 - a + lags - 1) // 4)
        got = jnp.dot(
            table[lowest * nb * 16 : (highest + 1) * nb * 16],
            toeplitz,
            preferred_element_type=F32,
        ).reshape(highest + 1 - lowest, nb, 2, 8, LANES)
        for quad in range(lowest, highest + 1):
            for h in range(2):
                place = a - (lags - 1) + 4 * quad + 2 * h
                if -1 <= place < frames:
                    term = got[quad - lowest, :, h]
                    old = total[place + 1]
                    total[place + 1] = term if old is None else old + term

    inside = (block < nblk - 1).astype(F32)
    pairs = nb // 2
    series = []
    for f in range(frames):
        line = []
        for j in range(pairs):
            both = []
            for b in (2 * j, 2 * j + 1):
                both.append(total[f + 1][b] + pltpu.roll(total[f][b], 4, 0))
            line.append(jnp.where(upper, both[0], pltpu.roll(both[1], 4, 0)))
            if f == frames - 1:
                line[-1] = line[-1] * inside
        series.append(line)

    height = rows * 8
    row = iota((height, LANES), 0)
    even = row % 8 < 4
    first_phase = row % 4 < 2
    for j in range(pairs):
        triple = jnp.concatenate(
            [
                jnp.concatenate([series[f + k][j] for f in range(rows)], axis=0)
                for k in range(3)
            ],
            axis=1,
        )
        centre = triple[:, LANES : 2 * LANES]
        high, low = split(triple)
        stacked = jnp.concatenate([high, low], axis=0)
        upper_table = rhi[4 * j : 4 * j + 4].reshape(4 * LANES, span)
        lower_table = rlo[4 * j : 4 * j + 4].reshape(4 * LANES, span)
        folded = nt_dot(stacked, upper_table)
        folded = folded[:height] + folded[height:] + nt_dot(high, lower_table)
        with_real = jnp.where(even, folded[:, :LANES], folded[:, 2 * LANES : 3 * LANES])
        with_imag = jnp.where(even, folded[:, LANES : 2 * LANES], folded[:, 3 * LANES :])
        corr = with_real + jnp.where(
            first_phase, pltpu.roll(with_imag, height - 2, 0), -pltpu.roll(with_imag, 2, 0)
        )
        square = triple * triple
        summed = nt_dot(jnp.concatenate(split(square), axis=0), ones_band)
        summed = summed[:height] + summed[height:]
        own = centre * centre
        lag = jnp.where(even, lag_energy[2 * j], lag_energy[2 * j + 1])
        value = summed - 2.0 * centre * corr + own * lag
        chi = (value + pltpu.roll(value, height - 2, 0)) / (2 * window + 1)
        energy = own + pltpu.roll(own, height - 2, 0)
        for f in range(rows):
            for half in range(2):
                at = 8 * f + 4 * half
                cols = slice(f * LANES, (f + 1) * LANES)
                out_sq[2 * j + half, :, cols] = energy[at : at + share]
                out_chi[2 * j + half, :, cols] = chi[at : at + share]

    for i in range(nr - 1):
        p_copy(core, lax.rem(core + i + 1, nr), i).wait_send()
    each(slots - 1, lambda i: x_copy(me, lax.rem(me + i + 1, slots), i).wait_send())
    each(peers - 1, lambda i: g_copy(mine, lax.rem(mine + i + 1, peers), i).wait_send())


def body(
    strain, gate_mask, psd_reset, psd_ref, psd_rate, filters, basis_count, mixing, autocorrelation
):
    nb, ntm, nr = lax.axis_size("bank"), lax.axis_size("tm"), lax.axis_size("rate")
    piece = strain.shape[1]
    rows = piece // LANES
    bin_rows = psd_ref.shape[1] // LANES
    basis, taps = filters.shape[2:]
    templ = mixing.shape[2]
    nblk = nb * ntm
    slots = nr * nblk
    group = min(16, slots)
    quads = taps // LANES // 4
    share = templ // nr
    pad = -(-(taps // LANES + 1) // rows) * rows
    constants = dft_constants(piece, group)
    vmem = pl.BlockSpec(memory_space=pltpu.VMEM)
    smem = pl.BlockSpec(memory_space=pltpu.SMEM)
    out = jax.ShapeDtypeStruct((nb, share, piece), F32)
    return pl.pallas_call(
        functools.partial(kernel, (nb, ntm, nr, group)),
        out_shape=(out, out),
        in_specs=[vmem, vmem, smem, vmem, vmem, vmem, smem, vmem, vmem] + [vmem] * 5,
        out_specs=(vmem, vmem),
        scratch_shapes=[
            pltpu.VMEM((slots, 2 * rows, LANES), F32),
            pltpu.VMEM((nr, 2 * bin_rows, LANES), F32),
            pltpu.VMEM((nr, quads, 16, LANES), BF16),
            pltpu.VMEM((nr, quads, nb, 16, LANES), BF16),
            pltpu.VMEM((nr, pad + nblk * rows + rows, LANES), F32),
            pltpu.VMEM((slots, rows, LANES), F32),
            pltpu.VMEM((slots, rows, LANES), F32),
            pltpu.VMEM((slots, rows, LANES), F32),
            pltpu.VMEM((2 * nb, 3 * LANES), F32),
            pltpu.VMEM((2 * nb, LANES, 3 * LANES), BF16),
            pltpu.VMEM((2 * nb, LANES, 3 * LANES), BF16),
            pltpu.SemaphoreType.DMA((slots,)),
            pltpu.SemaphoreType.DMA((slots,)),
            pltpu.SemaphoreType.DMA((nr,)),
            pltpu.SemaphoreType.DMA((nr,)),
            pltpu.SemaphoreType.DMA((nb * nr,)),
            pltpu.SemaphoreType.DMA((nb * nr,)),
        ],
        compiler_params=pltpu.CompilerParams(
            collective_id=0, has_side_effects=True, vmem_limit_bytes=40 * 1024 * 1024
        ),
    )(
        strain.reshape(rows, LANES),
        gate_mask.reshape(rows, LANES),
        psd_reset,
        psd_ref.reshape(bin_rows, LANES),
        psd_rate.reshape(bin_rows, LANES),
        filters.reshape(basis, taps),
        basis_count,
        mixing.reshape(templ * 2, basis),
        autocorrelation,
        *constants,
    )


def solution(mesh):
    return jax.shard_map(
        body,
        mesh=mesh,
        in_specs=(
            P("rate", ("parts", "bank", "tm")),
            P(("parts", "bank", "tm")),
            P(("parts", "bank", "tm")),
            P("rate", None),
            P("rate", None),
            P("bank", "rate", None, None),
            P("bank"),
            P("bank", "rate", None, None, None),
            P(),
        ),
        out_specs=(
            P(None, "rate", ("parts", "bank", "tm")),
            P(None, "rate", ("parts", "bank", "tm")),
        ),
        check_vma=False,
    )
```

```python
import functools

import jax
import jax.numpy as jnp
import numpy as np
from jax import lax
from jax.experimental import pallas as pl
from jax.experimental.pallas import tpu as pltpu
from jax.sharding import PartitionSpec as P

HIGHEST = lax.Precision.HIGHEST
F32 = jnp.float32
BF16 = jnp.bfloat16
LANES = 128
MESH = pl.DeviceIdType.MESH


def dft_constants(length, group):
    rows = length // LANES
    half = length // 2 // rows
    n1 = np.arange(rows)
    n2 = np.arange(LANES)
    small = 2.0 * np.pi * ((n1[:, None] * n1[None, :]) % rows) / rows
    eye = np.eye(group)
    first = np.concatenate([np.kron(eye, np.cos(small)), np.kron(eye, np.sin(small))], axis=0)
    last = np.concatenate([np.kron(eye, np.cos(small)), np.kron(eye, np.sin(small))], axis=1)
    angle = 2.0 * np.pi * (n1[:, None] * n2[None, :]) / length
    twiddle = np.stack([np.cos(angle), np.sin(angle)])
    wide = 2.0 * np.pi * ((n2[:, None] * n2[None, :]) % LANES) / LANES
    live = (n2 < half).astype(np.float64)
    c, s = np.cos(wide) * live, np.sin(wide) * live
    forward = np.concatenate(
        [np.concatenate([c, s], axis=1), np.concatenate([-s, c], axis=1)], axis=0
    )
    ct, st = c.T, s.T
    inverse = np.concatenate(
        [np.concatenate([ct, -st], axis=1), np.concatenate([st, ct], axis=1)], axis=0
    )
    return tuple(a.astype(np.float32) for a in (first, twiddle, forward, inverse, last))


def iota(shape, dim):
    return lax.broadcasted_iota(jnp.int32, shape, dim)


def each(count, step):
    if count <= 32:
        for i in range(count):
            step(i)
    else:
        lax.fori_loop(0, count, lambda i, c: (step(i), c)[1], 0)


def split(x):
    high = x.astype(BF16)
    return high, (x - high.astype(F32)).astype(BF16)


def nt_dot(a, b):
    return lax.dot_general(a, b, (((1,), (1,)), ((), ())), preferred_element_type=F32)


def kernel(sizes, *refs):
    sources, (out_sq, out_chi), held = refs[:14], refs[14:16], refs[16:30]
    strain, gate, reset, ref, rate, filters, count, mixing, auto = held[:9]
    first, twiddle, forward, inverse, last = held[9:]
    (xbuf, pbuf, gsend, gbuf, wbuf, lbuf, yre, yim, rpad, rhi, rlo) = refs[30:41]
    (x_send, x_recv, p_send, p_recv, g_send, g_recv, in_sem) = refs[41:]
    loads = [
        pltpu.make_async_copy(source, target, in_sem.at[i])
        for i, (source, target) in enumerate(zip(sources, held))
    ]
    for load in loads:
        load.start()
    nb, ntm, nr, group = sizes
    nblk = nb * ntm
    slots = nr * nblk
    rows = xbuf.shape[1] // 2
    taps = filters.shape[1]
    lags = taps // LANES
    bank, tm, core = lax.axis_index("bank"), lax.axis_index("tm"), lax.axis_index("rate")
    block = bank * ntm + tm
    me = core * nblk + block

    def device(slot):
        blk = lax.rem(slot, nblk)
        return {"bank": blk // ntm, "tm": lax.rem(blk, ntm), "rate": slot // nblk}

    barrier = pltpu.get_barrier_semaphore()

    def greet(i):
        pl.semaphore_signal(
            barrier, inc=1, device_id=device(lax.rem(me + i + 1, slots)), device_id_type=MESH
        )

    each(slots - 1, greet)

    for load in loads[:5]:
        load.wait()
    xbuf[me, 0:rows, :] = strain[...] * gate[...].astype(F32)
    xbuf[me, rows : 2 * rows, :] = jnp.full((rows, LANES), reset[0], jnp.int32).astype(F32)
    bin_rows = ref.shape[0]
    pbuf[core, 0:bin_rows, :] = ref[...]
    pbuf[core, bin_rows : 2 * bin_rows, :] = rate[...]

    pl.semaphore_wait(barrier, slots - 1)

    def x_copy(src_slot, target, i):
        return pltpu.make_async_remote_copy(
            src_ref=xbuf.at[src_slot],
            dst_ref=xbuf.at[src_slot],
            send_sem=x_send.at[i],
            recv_sem=x_recv.at[src_slot],
            device_id=device(target),
            device_id_type=MESH,
        )

    def p_copy(src_core, target, i):
        return pltpu.make_async_remote_copy(
            src_ref=pbuf.at[src_core],
            dst_ref=pbuf.at[src_core],
            send_sem=p_send.at[i],
            recv_sem=p_recv.at[src_core],
            device_id={"rate": target},
            device_id_type=MESH,
        )

    each(slots - 1, lambda i: x_copy(me, lax.rem(me + i + 1, slots), i).start())
    for i in range(nr - 1):
        p_copy(core, lax.rem(core + i + 1, nr), i).start()

    for load in loads[5:]:
        load.wait()
    basis = filters.shape[0]
    mix_rows = mixing.shape[0]
    share = mix_rows // nr // 2
    live = (iota((mix_rows, basis), 1) < count[0]).astype(F32)
    dest, source = iota((mix_rows, mix_rows), 0), iota((mix_rows, mix_rows), 1)
    inner = dest % (2 * share)
    wanted = dest // (2 * share) * (2 * share) + inner % share * 2 + inner // share
    perm = (source == wanted).astype(F32)
    mixed_rows = jnp.dot(perm, mixing[...].astype(F32) * live, preferred_element_type=F32)
    mixed = jnp.dot(mixed_rows.astype(BF16), filters[...], preferred_element_type=F32)
    upper = iota((8, LANES), 0) < 4
    for r in range(nr):
        for quad in range(lags // 4):
            parts = []
            for h in range(2):
                at = (4 * quad + 2 * h) * LANES
                low, high = mixed[:, at : at + LANES], mixed[:, at + LANES : at + 2 * LANES]
                if r == 0:
                    high = pltpu.roll(high, 4, 0)
                else:
                    low = pltpu.roll(low, 4, 0)
                parts.append(jnp.where(upper, low, high))
            gsend[r, quad] = jnp.concatenate(parts, axis=0).astype(BF16)

    peers = nb * nr
    mine = core * nb + bank

    def g_copy(source, target, i):
        return pltpu.make_async_remote_copy(
            src_ref=gsend.at[target // nb],
            dst_ref=gbuf.at[source // nb, :, lax.rem(source, nb)],
            send_sem=g_send.at[i],
            recv_sem=g_recv.at[source],
            device_id={"bank": lax.rem(target, nb), "rate": target // nb},
            device_id_type=MESH,
        )

    each(peers - 1, lambda i: g_copy(mine, lax.rem(mine + i + 1, peers), i).start())
    gbuf[core, :, bank] = gsend[core]

    window = auto.shape[2] // 2
    span = 3 * LANES
    rpad[...] = jnp.zeros_like(rpad)
    for b in range(nb):
        for d in range(2):
            rpad[2 * b + d : 2 * b + d + 1, 0 : auto.shape[2]] = auto[b, d : d + 1, :]
    lag_energy = []
    for b in range(nb):
        series = rpad[2 * b : 2 * b + 2, :]
        lag_energy.append(jnp.sum(series * series, keepdims=True))

    def band(row):
        line = jnp.broadcast_to(rpad[pl.ds(row, 1), :], (LANES, span))
        high, low = split(pltpu.roll(line, 0, 1, stride=1, stride_axis=0))
        rhi[row] = high
        rlo[row] = low

    each(2 * nb, band)
    offset = iota((LANES, span), 1) - iota((LANES, span), 0)
    ones_band = ((offset >= 0) & (offset <= 2 * window)).astype(F32).astype(BF16)

    for i in range(nr - 1):
        p_copy(lax.rem(core + i + 1, nr), core, i).wait_recv()
    each(slots - 1, lambda i: x_copy(lax.rem(me + i + 1, slots), me, i).wait_recv())

    bins = bin_rows * LANES
    pick = iota((rows, LANES), 1) % rows == iota((rows, LANES), 0)
    lines = []
    for c in range(nr):
        for which in range(2):
            pieces = []
            for q in range(bin_rows):
                row = pbuf[c, which * bin_rows + q : which * bin_rows + q + 1, :]
                pieces.append(jnp.where(pick, jnp.broadcast_to(row, (rows, LANES)), 0.0))
            lines.append(jnp.concatenate(pieces, axis=1))
    gather = (iota((bins, LANES), 0) // rows == iota((bins, LANES), 1)).astype(F32)
    psd = jnp.dot(
        jnp.concatenate(lines, axis=0), gather, precision=HIGHEST, preferred_element_type=F32
    )
    lane = iota((rows, LANES), 1)
    live_bin = lane < bins // rows
    length = rows * LANES
    weight = jnp.where(
        live_bin,
        jnp.where((lane == 0) & (iota((rows, LANES), 0) == 0), 1.0 / length, 2.0 / length),
        0.0,
    )
    levels = [jnp.where(live_bin, psd[2 * c * rows : (2 * c + 1) * rows], 1.0) for c in range(nr)]
    rates = [psd[(2 * c + 1) * rows : (2 * c + 2) * rows] for c in range(nr)]

    tall = group * rows
    cos_tw = jnp.broadcast_to(twiddle[0][None], (group, rows, LANES)).reshape(tall, LANES)
    sin_tw = jnp.broadcast_to(twiddle[1][None], (group, rows, LANES)).reshape(tall, LANES)
    for s in range(slots // group):
        x = xbuf[s * group : (s + 1) * group, 0:rows, :].reshape(tall, LANES)
        y = jnp.dot(first[...], x, precision=HIGHEST, preferred_element_type=F32)
        a, b = y[:tall], y[tall:]
        turned = jnp.concatenate([a * cos_tw - b * sin_tw, a * sin_tw + b * cos_tw], axis=1)
        spec = jnp.dot(turned, forward[...], precision=HIGHEST, preferred_element_type=F32)
        real, imag = spec[:, :LANES], spec[:, LANES:]
        yre[s * group : (s + 1) * group] = real.reshape(group, rows, LANES)
        yim[s * group : (s + 1) * group] = imag.reshape(group, rows, LANES)
        power = (real * real + imag * imag) / (length / 2)
        lbuf[s * group : (s + 1) * group] = power.reshape(group, rows, LANES)

    def advance(i, states):
        after = []
        for c in range(nr):
            at = c * nblk + i
            keep = (1.0 - rates[c]) * (1.0 - 0.5 * xbuf[at, rows : 2 * rows, :])
            level = jnp.log(lbuf[at] + 0.1 * levels[c])
            state = keep * states[c] + rates[c] * level
            lbuf[at] = jnp.exp(-0.5 * state) * weight
            after.append(state)
        return tuple(after)

    states = tuple(jnp.log(levels[c]) for c in range(nr))
    if nblk <= 16:
        for i in range(nblk):
            states = advance(i, states)
    else:
        lax.fori_loop(0, nblk, advance, states)

    pad = wbuf.shape[1] - nblk * rows - rows
    for c in range(nr):
        wbuf[c, 0:pad, :] = jnp.zeros((pad, LANES), F32)
        wbuf[c, pad + nblk * rows :, :] = jnp.zeros((rows, LANES), F32)
    per_copy = min(group, nblk)
    for s in range(slots // group):
        scale = lbuf[s * group : (s + 1) * group].reshape(tall, LANES)
        real = yre[s * group : (s + 1) * group].reshape(tall, LANES) * scale
        imag = yim[s * group : (s + 1) * group].reshape(tall, LANES) * scale
        y = jnp.dot(
            jnp.concatenate([real, imag], axis=1),
            inverse[...],
            precision=HIGHEST,
            preferred_element_type=F32,
        )
        a, b = y[:, :LANES], y[:, LANES:]
        turned = jnp.concatenate([a * cos_tw + b * sin_tw, b * cos_tw - a * sin_tw], axis=0)
        white = jnp.dot(last[...], turned, precision=HIGHEST, preferred_element_type=F32)
        white = white.astype(BF16).astype(F32)
        for piece in range(group // per_copy):
            slot = s * group + piece * per_copy
            c, blk = slot // nblk, slot % nblk
            at = pad + blk * rows
            wbuf[c, at : at + per_copy * rows, :] = white[
                piece * per_copy * rows : (piece + 1) * per_copy * rows
            ]

    each(peers - 1, lambda i: g_copy(lax.rem(mine + i + 1, peers), mine, i).wait_recv())
    frames = rows + 2
    start = pl.multiple_of(block * rows, rows)
    view = [wbuf[c, pl.ds(start, pad + 2 * rows), :] for c in range(nr)]
    quads = lags // 4
    table = jnp.concatenate(
        [gbuf[c].reshape(quads * nb * 16, LANES) for c in range(nr)], axis=1
    )
    later = iota((LANES, LANES), 1) >= iota((LANES, LANES), 0)

    def spun(c, row):
        line = jnp.broadcast_to(view[c][row : row + 1, :], (LANES, LANES))
        return pltpu.roll(line, 0, 1, stride=1, stride_axis=0)

    total = [None] * (frames + 1)
    before = [spun(c, pad - lags - 1) for c in range(nr)]
    for a in range(frames + lags - 1):
        now = [spun(c, pad - lags + a) for c in range(nr)]
        toeplitz = jnp.concatenate(
            [jnp.where(later, now[c], before[c]).astype(BF16) for c in range(nr)], axis=0
        )
        before = now
        lowest = max(0, -((a - lags + 4) // 4))
        highest = min(quads - 1, (frames - 1 - a + lags - 1) // 4)
        got = jnp.dot(
            table[lowest * nb * 16 : (highest + 1) * nb * 16],
            toeplitz,
            preferred_element_type=F32,
        ).reshape(highest + 1 - lowest, nb, 2, 8, LANES)
        for quad in range(lowest, highest + 1):
            for h in range(2):
                place = a - (lags - 1) + 4 * quad + 2 * h
                if -1 <= place < frames:
                    term = got[quad - lowest, :, h]
                    old = total[place + 1]
                    total[place + 1] = term if old is None else old + term

    inside = (block < nblk - 1).astype(F32)
    pairs = nb // 2
    series = []
    for f in range(frames):
        line = []
        for j in range(pairs):
            both = []
            for b in (2 * j, 2 * j + 1):
                both.append(total[f + 1][b] + pltpu.roll(total[f][b], 4, 0))
            line.append(jnp.where(upper, both[0], pltpu.roll(both[1], 4, 0)))
            if f == frames - 1:
                line[-1] = line[-1] * inside
        series.append(line)

    height = rows * 8
    row = iota((height, LANES), 0)
    even = row % 8 < 4
    first_phase = row % 4 < 2
    for j in range(pairs):
        triple = jnp.concatenate(
            [
                jnp.concatenate([series[f + k][j] for f in range(rows)], axis=0)
                for k in range(3)
            ],
            axis=1,
        )
        centre = triple[:, LANES : 2 * LANES]
        high, low = split(triple)
        stacked = jnp.concatenate([high, low], axis=0)
        upper_table = rhi[4 * j : 4 * j + 4].reshape(4 * LANES, span)
        lower_table = rlo[4 * j : 4 * j + 4].reshape(4 * LANES, span)
        folded = nt_dot(stacked, upper_table)
        folded = folded[:height] + folded[height:] + nt_dot(high, lower_table)
        with_real = jnp.where(even, folded[:, :LANES], folded[:, 2 * LANES : 3 * LANES])
        with_imag = jnp.where(even, folded[:, LANES : 2 * LANES], folded[:, 3 * LANES :])
        corr = with_real + jnp.where(
            first_phase, pltpu.roll(with_imag, height - 2, 0), -pltpu.roll(with_imag, 2, 0)
        )
        square = triple * triple
        summed = nt_dot(jnp.concatenate(split(square), axis=0), ones_band)
        summed = summed[:height] + summed[height:]
        own = centre * centre
        lag = jnp.where(even, lag_energy[2 * j], lag_energy[2 * j + 1])
        value = summed - 2.0 * centre * corr + own * lag
        chi = (value + pltpu.roll(value, height - 2, 0)) / (2 * window + 1)
        energy = own + pltpu.roll(own, height - 2, 0)
        for f in range(rows):
            for half in range(2):
                at = 8 * f + 4 * half
                cols = slice(f * LANES, (f + 1) * LANES)
                out_sq[2 * j + half, :, cols] = energy[at : at + share]
                out_chi[2 * j + half, :, cols] = chi[at : at + share]

    for i in range(nr - 1):
        p_copy(core, lax.rem(core + i + 1, nr), i).wait_send()
    each(slots - 1, lambda i: x_copy(me, lax.rem(me + i + 1, slots), i).wait_send())
    each(peers - 1, lambda i: g_copy(mine, lax.rem(mine + i + 1, peers), i).wait_send())


def body(
    strain, gate_mask, psd_reset, psd_ref, psd_rate, filters, basis_count, mixing, autocorrelation
):
    nb, ntm, nr = lax.axis_size("bank"), lax.axis_size("tm"), lax.axis_size("rate")
    piece = strain.shape[1]
    rows = piece // LANES
    bin_rows = psd_ref.shape[1] // LANES
    basis, taps = filters.shape[2:]
    templ = mixing.shape[2]
    nblk = nb * ntm
    slots = nr * nblk
    group = min(16, slots)
    quads = taps // LANES // 4
    share = templ // nr
    pad = -(-(taps // LANES + 1) // rows) * rows
    constants = dft_constants(piece, group)
    vmem = pl.BlockSpec(memory_space=pltpu.VMEM)
    out = jax.ShapeDtypeStruct((nb, share, piece), F32)
    operands = (
        strain.reshape(rows, LANES),
        gate_mask.reshape(rows, LANES),
        psd_reset,
        psd_ref.reshape(bin_rows, LANES),
        psd_rate.reshape(bin_rows, LANES),
        filters.reshape(basis, taps),
        basis_count,
        mixing.reshape(templ * 2, basis),
        autocorrelation,
        *constants,
    )
    held = [(pltpu.SMEM if a.ndim == 1 else pltpu.VMEM)(a.shape, a.dtype) for a in operands]
    return pl.pallas_call(
        functools.partial(kernel, (nb, ntm, nr, group)),
        out_shape=(out, out),
        in_specs=[pl.BlockSpec(memory_space=pltpu.HBM)] * len(operands),
        out_specs=(vmem, vmem),
        scratch_shapes=held
        + [
            pltpu.VMEM((slots, 2 * rows, LANES), F32),
            pltpu.VMEM((nr, 2 * bin_rows, LANES), F32),
            pltpu.VMEM((nr, quads, 16, LANES), BF16),
            pltpu.VMEM((nr, quads, nb, 16, LANES), BF16),
            pltpu.VMEM((nr, pad + nblk * rows + rows, LANES), F32),
            pltpu.VMEM((slots, rows, LANES), F32),
            pltpu.VMEM((slots, rows, LANES), F32),
            pltpu.VMEM((slots, rows, LANES), F32),
            pltpu.VMEM((2 * nb, 3 * LANES), F32),
            pltpu.VMEM((2 * nb, LANES, 3 * LANES), BF16),
            pltpu.VMEM((2 * nb, LANES, 3 * LANES), BF16),
            pltpu.SemaphoreType.DMA((slots,)),
            pltpu.SemaphoreType.DMA((slots,)),
            pltpu.SemaphoreType.DMA((nr,)),
            pltpu.SemaphoreType.DMA((nr,)),
            pltpu.SemaphoreType.DMA((nb * nr,)),
            pltpu.SemaphoreType.DMA((nb * nr,)),
            pltpu.SemaphoreType.DMA((len(operands),)),
        ],
        compiler_params=pltpu.CompilerParams(
            collective_id=0, has_side_effects=True, vmem_limit_bytes=62 * 1024 * 1024
        ),
    )(*operands)


def solution(mesh):
    return jax.shard_map(
        body,
        mesh=mesh,
        in_specs=(
            P("rate", ("parts", "bank", "tm")),
            P(("parts", "bank", "tm")),
            P(("parts", "bank", "tm")),
            P("rate", None),
            P("rate", None),
            P("bank", "rate", None, None),
            P("bank"),
            P("bank", "rate", None, None, None),
            P(),
        ),
        out_specs=(
            P(None, "rate", ("parts", "bank", "tm")),
            P(None, "rate", ("parts", "bank", "tm")),
        ),
        check_vma=False,
    )
```

```python
import functools

import jax
import jax.numpy as jnp
import numpy as np
from jax import lax
from jax.experimental import pallas as pl
from jax.experimental.pallas import tpu as pltpu
from jax.sharding import PartitionSpec as P

HIGHEST = lax.Precision.HIGHEST
F32 = jnp.float32
BF16 = jnp.bfloat16
LANES = 128
MESH = pl.DeviceIdType.MESH


def dft_constants(length, group):
    rows = length // LANES
    half = length // 2 // rows
    n1 = np.arange(rows)
    n2 = np.arange(LANES)
    small = 2.0 * np.pi * ((n1[:, None] * n1[None, :]) % rows) / rows
    eye = np.eye(group)
    first = np.concatenate([np.kron(eye, np.cos(small)), np.kron(eye, np.sin(small))], axis=0)
    last = np.concatenate([np.kron(eye, np.cos(small)), np.kron(eye, np.sin(small))], axis=1)
    angle = 2.0 * np.pi * (n1[:, None] * n2[None, :]) / length
    twiddle = np.stack([np.cos(angle), np.sin(angle)])
    wide = 2.0 * np.pi * ((n2[:, None] * n2[None, :]) % LANES) / LANES
    live = (n2 < half).astype(np.float64)
    c, s = np.cos(wide) * live, np.sin(wide) * live
    forward = np.concatenate(
        [np.concatenate([c, s], axis=1), np.concatenate([-s, c], axis=1)], axis=0
    )
    ct, st = c.T, s.T
    inverse = np.concatenate(
        [np.concatenate([ct, -st], axis=1), np.concatenate([st, ct], axis=1)], axis=0
    )
    return tuple(a.astype(np.float32) for a in (first, twiddle, forward, inverse, last))


def iota(shape, dim):
    return lax.broadcasted_iota(jnp.int32, shape, dim)


def each(count, step):
    if count <= 32:
        for i in range(count):
            step(i)
    else:
        lax.fori_loop(0, count, lambda i, c: (step(i), c)[1], 0)


def split(x):
    high = x.astype(BF16)
    return high, (x - high.astype(F32)).astype(BF16)


def nt_dot(a, b):
    return lax.dot_general(a, b, (((1,), (1,)), ((), ())), preferred_element_type=F32)


def kernel(sizes, *refs):
    sources, out, held = refs[:14], refs[14], refs[15:29]
    strain, gate, reset, ref, rate, filters, count, mixing, auto = held[:9]
    first, twiddle, forward, inverse, last = held[9:]
    (xbuf, pbuf, gsend, gbuf, wbuf, lbuf, yre, yim, rpad, rhi, rlo) = refs[29:40]
    (x_send, x_recv, p_send, p_recv, g_send, g_recv, in_sem) = refs[40:]
    loads = [
        pltpu.make_async_copy(source, target, in_sem.at[i])
        for i, (source, target) in enumerate(zip(sources, held))
    ]
    for load in loads:
        load.start()
    nb, ntm, nr, group = sizes
    nblk = nb * ntm
    slots = nr * nblk
    rows = xbuf.shape[1] // 2
    taps = filters.shape[1]
    lags = taps // LANES
    bank, tm, core = lax.axis_index("bank"), lax.axis_index("tm"), lax.axis_index("rate")
    block = bank * ntm + tm
    me = core * nblk + block

    def device(slot):
        blk = lax.rem(slot, nblk)
        return {"bank": blk // ntm, "tm": lax.rem(blk, ntm), "rate": slot // nblk}

    barrier = pltpu.get_barrier_semaphore()

    def greet(i):
        pl.semaphore_signal(
            barrier, inc=1, device_id=device(lax.rem(me + i + 1, slots)), device_id_type=MESH
        )

    each(slots - 1, greet)

    for load in loads[:5]:
        load.wait()
    xbuf[me, 0:rows, :] = strain[...] * gate[...].astype(F32)
    xbuf[me, rows : 2 * rows, :] = jnp.full((rows, LANES), reset[0], jnp.int32).astype(F32)
    bin_rows = ref.shape[0]
    pbuf[core, 0:bin_rows, :] = ref[...]
    pbuf[core, bin_rows : 2 * bin_rows, :] = rate[...]

    pl.semaphore_wait(barrier, slots - 1)

    def x_copy(src_slot, target, i):
        return pltpu.make_async_remote_copy(
            src_ref=xbuf.at[src_slot],
            dst_ref=xbuf.at[src_slot],
            send_sem=x_send.at[i],
            recv_sem=x_recv.at[src_slot],
            device_id=device(target),
            device_id_type=MESH,
        )

    def p_copy(src_core, target, i):
        return pltpu.make_async_remote_copy(
            src_ref=pbuf.at[src_core],
            dst_ref=pbuf.at[src_core],
            send_sem=p_send.at[i],
            recv_sem=p_recv.at[src_core],
            device_id={"rate": target},
            device_id_type=MESH,
        )

    each(slots - 1, lambda i: x_copy(me, lax.rem(me + i + 1, slots), i).start())
    for i in range(nr - 1):
        p_copy(core, lax.rem(core + i + 1, nr), i).start()

    for load in loads[5:]:
        load.wait()
    basis = filters.shape[0]
    mix_rows = mixing.shape[0]
    share = mix_rows // nr // 2
    live = (iota((mix_rows, basis), 1) < count[0]).astype(F32)
    dest, source = iota((mix_rows, mix_rows), 0), iota((mix_rows, mix_rows), 1)
    inner = dest % (2 * share)
    wanted = dest // (2 * share) * (2 * share) + inner % share * 2 + inner // share
    perm = (source == wanted).astype(F32)
    mixed_rows = jnp.dot(perm, mixing[...].astype(F32) * live, preferred_element_type=F32)
    mixed = jnp.dot(mixed_rows.astype(BF16), filters[...], preferred_element_type=F32)
    upper = iota((8, LANES), 0) < 4
    for r in range(nr):
        for quad in range(lags // 4):
            parts = []
            for h in range(2):
                at = (4 * quad + 2 * h) * LANES
                low, high = mixed[:, at : at + LANES], mixed[:, at + LANES : at + 2 * LANES]
                if r == 0:
                    high = pltpu.roll(high, 4, 0)
                else:
                    low = pltpu.roll(low, 4, 0)
                parts.append(jnp.where(upper, low, high))
            gsend[r, quad] = jnp.concatenate(parts, axis=0).astype(BF16)

    peers = nb * nr
    mine = core * nb + bank

    def g_copy(source, target, i):
        return pltpu.make_async_remote_copy(
            src_ref=gsend.at[target // nb],
            dst_ref=gbuf.at[source // nb, :, lax.rem(source, nb)],
            send_sem=g_send.at[i],
            recv_sem=g_recv.at[source],
            device_id={"bank": lax.rem(target, nb), "rate": target // nb},
            device_id_type=MESH,
        )

    each(peers - 1, lambda i: g_copy(mine, lax.rem(mine + i + 1, peers), i).start())
    gbuf[core, :, bank] = gsend[core]

    window = auto.shape[2] // 2
    span = 3 * LANES
    rpad[...] = jnp.zeros_like(rpad)
    for b in range(nb):
        for d in range(2):
            rpad[2 * b + d : 2 * b + d + 1, 0 : auto.shape[2]] = auto[b, d : d + 1, :]
    lag_energy = []
    for b in range(nb):
        series = rpad[2 * b : 2 * b + 2, :]
        lag_energy.append(jnp.sum(series * series, keepdims=True))

    def band(row):
        line = jnp.broadcast_to(rpad[pl.ds(row, 1), :], (LANES, span))
        high, low = split(pltpu.roll(line, 0, 1, stride=1, stride_axis=0))
        rhi[row] = high
        rlo[row] = low

    each(2 * nb, band)
    offset = iota((LANES, span), 1) - iota((LANES, span), 0)
    ones_band = ((offset >= 0) & (offset <= 2 * window)).astype(F32).astype(BF16)

    for i in range(nr - 1):
        p_copy(lax.rem(core + i + 1, nr), core, i).wait_recv()
    each(slots - 1, lambda i: x_copy(lax.rem(me + i + 1, slots), me, i).wait_recv())

    bins = bin_rows * LANES
    pick = iota((rows, LANES), 1) % rows == iota((rows, LANES), 0)
    lines = []
    for c in range(nr):
        for which in range(2):
            pieces = []
            for q in range(bin_rows):
                row = pbuf[c, which * bin_rows + q : which * bin_rows + q + 1, :]
                pieces.append(jnp.where(pick, jnp.broadcast_to(row, (rows, LANES)), 0.0))
            lines.append(jnp.concatenate(pieces, axis=1))
    gather = (iota((bins, LANES), 0) // rows == iota((bins, LANES), 1)).astype(F32)
    psd = jnp.dot(
        jnp.concatenate(lines, axis=0), gather, precision=HIGHEST, preferred_element_type=F32
    )
    lane = iota((rows, LANES), 1)
    live_bin = lane < bins // rows
    length = rows * LANES
    weight = jnp.where(
        live_bin,
        jnp.where((lane == 0) & (iota((rows, LANES), 0) == 0), 1.0 / length, 2.0 / length),
        0.0,
    )
    levels = [jnp.where(live_bin, psd[2 * c * rows : (2 * c + 1) * rows], 1.0) for c in range(nr)]
    rates = [psd[(2 * c + 1) * rows : (2 * c + 2) * rows] for c in range(nr)]

    tall = group * rows
    cos_tw = jnp.broadcast_to(twiddle[0][None], (group, rows, LANES)).reshape(tall, LANES)
    sin_tw = jnp.broadcast_to(twiddle[1][None], (group, rows, LANES)).reshape(tall, LANES)
    for s in range(slots // group):
        x = xbuf[s * group : (s + 1) * group, 0:rows, :].reshape(tall, LANES)
        y = jnp.dot(first[...], x, precision=HIGHEST, preferred_element_type=F32)
        a, b = y[:tall], y[tall:]
        turned = jnp.concatenate([a * cos_tw - b * sin_tw, a * sin_tw + b * cos_tw], axis=1)
        spec = jnp.dot(turned, forward[...], precision=HIGHEST, preferred_element_type=F32)
        real, imag = spec[:, :LANES], spec[:, LANES:]
        yre[s * group : (s + 1) * group] = real.reshape(group, rows, LANES)
        yim[s * group : (s + 1) * group] = imag.reshape(group, rows, LANES)
        power = (real * real + imag * imag) / (length / 2)
        lbuf[s * group : (s + 1) * group] = power.reshape(group, rows, LANES)

    def advance(i, states):
        after = []
        for c in range(nr):
            at = c * nblk + i
            keep = (1.0 - rates[c]) * (1.0 - 0.5 * xbuf[at, rows : 2 * rows, :])
            level = jnp.log(lbuf[at] + 0.1 * levels[c])
            state = keep * states[c] + rates[c] * level
            lbuf[at] = jnp.exp(-0.5 * state) * weight
            after.append(state)
        return tuple(after)

    states = tuple(jnp.log(levels[c]) for c in range(nr))
    if nblk <= 16:
        for i in range(nblk):
            states = advance(i, states)
    else:
        lax.fori_loop(0, nblk, advance, states)

    pad = wbuf.shape[1] - nblk * rows - rows
    for c in range(nr):
        wbuf[c, 0:pad, :] = jnp.zeros((pad, LANES), F32)
        wbuf[c, pad + nblk * rows :, :] = jnp.zeros((rows, LANES), F32)
    per_copy = min(group, nblk)
    for s in range(slots // group):
        scale = lbuf[s * group : (s + 1) * group].reshape(tall, LANES)
        real = yre[s * group : (s + 1) * group].reshape(tall, LANES) * scale
        imag = yim[s * group : (s + 1) * group].reshape(tall, LANES) * scale
        y = jnp.dot(
            jnp.concatenate([real, imag], axis=1),
            inverse[...],
            precision=HIGHEST,
            preferred_element_type=F32,
        )
        a, b = y[:, :LANES], y[:, LANES:]
        turned = jnp.concatenate([a * cos_tw + b * sin_tw, b * cos_tw - a * sin_tw], axis=0)
        white = jnp.dot(last[...], turned, precision=HIGHEST, preferred_element_type=F32)
        white = white.astype(BF16).astype(F32)
        for piece in range(group // per_copy):
            slot = s * group + piece * per_copy
            c, blk = slot // nblk, slot % nblk
            at = pad + blk * rows
            wbuf[c, at : at + per_copy * rows, :] = white[
                piece * per_copy * rows : (piece + 1) * per_copy * rows
            ]

    each(peers - 1, lambda i: g_copy(lax.rem(mine + i + 1, peers), mine, i).wait_recv())
    frames = rows + 2
    start = pl.multiple_of(block * rows, rows)
    view = [wbuf[c, pl.ds(start, pad + 2 * rows), :] for c in range(nr)]
    quads = lags // 4
    table = jnp.concatenate(
        [gbuf[c].reshape(quads * nb * 16, LANES) for c in range(nr)], axis=1
    )
    later = iota((LANES, LANES), 1) >= iota((LANES, LANES), 0)

    def spun(c, row):
        line = jnp.broadcast_to(view[c][row : row + 1, :], (LANES, LANES))
        return pltpu.roll(line, 0, 1, stride=1, stride_axis=0)

    total = [None] * (frames + 1)
    before = [spun(c, pad - lags - 1) for c in range(nr)]
    for a in range(frames + lags - 1):
        now = [spun(c, pad - lags + a) for c in range(nr)]
        toeplitz = jnp.concatenate(
            [jnp.where(later, now[c], before[c]).astype(BF16) for c in range(nr)], axis=0
        )
        before = now
        lowest = max(0, -((a - lags + 4) // 4))
        highest = min(quads - 1, (frames - 1 - a + lags - 1) // 4)
        got = jnp.dot(
            table[lowest * nb * 16 : (highest + 1) * nb * 16],
            toeplitz,
            preferred_element_type=F32,
        ).reshape(highest + 1 - lowest, nb, 2, 8, LANES)
        for quad in range(lowest, highest + 1):
            for h in range(2):
                place = a - (lags - 1) + 4 * quad + 2 * h
                if -1 <= place < frames:
                    term = got[quad - lowest, :, h]
                    old = total[place + 1]
                    total[place + 1] = term if old is None else old + term

    inside = (block < nblk - 1).astype(F32)
    pairs = nb // 2
    series = []
    for f in range(frames):
        line = []
        for j in range(pairs):
            both = []
            for b in (2 * j, 2 * j + 1):
                both.append(total[f + 1][b] + pltpu.roll(total[f][b], 4, 0))
            line.append(jnp.where(upper, both[0], pltpu.roll(both[1], 4, 0)))
            if f == frames - 1:
                line[-1] = line[-1] * inside
        series.append(line)

    height = rows * 8
    row = iota((height, LANES), 0)
    even = row % 8 < 4
    first_phase = row % 4 < 2
    for j in range(pairs):
        triple = jnp.concatenate(
            [
                jnp.concatenate([series[f + k][j] for f in range(rows)], axis=0)
                for k in range(3)
            ],
            axis=1,
        )
        centre = triple[:, LANES : 2 * LANES]
        high, low = split(triple)
        stacked = jnp.concatenate([high, low], axis=0)
        upper_table = rhi[4 * j : 4 * j + 4].reshape(4 * LANES, span)
        lower_table = rlo[4 * j : 4 * j + 4].reshape(4 * LANES, span)
        folded = nt_dot(stacked, upper_table)
        folded = folded[:height] + folded[height:] + nt_dot(high, lower_table)
        with_real = jnp.where(even, folded[:, :LANES], folded[:, 2 * LANES : 3 * LANES])
        with_imag = jnp.where(even, folded[:, LANES : 2 * LANES], folded[:, 3 * LANES :])
        corr = with_real + jnp.where(
            first_phase, pltpu.roll(with_imag, height - 2, 0), -pltpu.roll(with_imag, 2, 0)
        )
        square = triple * triple
        summed = nt_dot(jnp.concatenate(split(square), axis=0), ones_band)
        summed = summed[:height] + summed[height:]
        own = centre * centre
        lag = jnp.where(even, lag_energy[2 * j], lag_energy[2 * j + 1])
        value = summed - 2.0 * centre * corr + own * lag
        chi = value + pltpu.roll(value, height - 2, 0)
        energy = own + pltpu.roll(own, height - 2, 0)
        for f in range(rows):
            for half in range(2):
                at = 8 * f + 4 * half
                cols = slice(f * LANES, (f + 1) * LANES)
                out[0, 2 * j + half, :, cols] = energy[at : at + share]
                out[1, 2 * j + half, :, cols] = chi[at : at + share]

    for i in range(nr - 1):
        p_copy(core, lax.rem(core + i + 1, nr), i).wait_send()
    each(slots - 1, lambda i: x_copy(me, lax.rem(me + i + 1, slots), i).wait_send())
    each(peers - 1, lambda i: g_copy(mine, lax.rem(mine + i + 1, peers), i).wait_send())


def body(
    strain, gate_mask, psd_reset, psd_ref, psd_rate, filters, basis_count, mixing, autocorrelation
):
    nb, ntm, nr = lax.axis_size("bank"), lax.axis_size("tm"), lax.axis_size("rate")
    piece = strain.shape[1]
    rows = piece // LANES
    bin_rows = psd_ref.shape[1] // LANES
    basis, taps = filters.shape[2:]
    templ = mixing.shape[2]
    nblk = nb * ntm
    slots = nr * nblk
    group = min(16, slots)
    quads = taps // LANES // 4
    share = templ // nr
    pad = -(-(taps // LANES + 1) // rows) * rows
    constants = dft_constants(piece, group)
    vmem = pl.BlockSpec(memory_space=pltpu.VMEM)
    out = jax.ShapeDtypeStruct((2, nb, share, piece), F32)
    operands = (
        strain.reshape(rows, LANES),
        gate_mask.reshape(rows, LANES),
        psd_reset,
        psd_ref.reshape(bin_rows, LANES),
        psd_rate.reshape(bin_rows, LANES),
        filters.reshape(basis, taps),
        basis_count,
        mixing.reshape(templ * 2, basis),
        autocorrelation,
        *constants,
    )
    held = [(pltpu.SMEM if a.ndim == 1 else pltpu.VMEM)(a.shape, a.dtype) for a in operands]
    both = pl.pallas_call(
        functools.partial(kernel, (nb, ntm, nr, group)),
        out_shape=out,
        in_specs=[pl.BlockSpec(memory_space=pltpu.HBM)] * len(operands),
        out_specs=vmem,
        scratch_shapes=held
        + [
            pltpu.VMEM((slots, 2 * rows, LANES), F32),
            pltpu.VMEM((nr, 2 * bin_rows, LANES), F32),
            pltpu.VMEM((nr, quads, 16, LANES), BF16),
            pltpu.VMEM((nr, quads, nb, 16, LANES), BF16),
            pltpu.VMEM((nr, pad + nblk * rows + rows, LANES), F32),
            pltpu.VMEM((slots, rows, LANES), F32),
            pltpu.VMEM((slots, rows, LANES), F32),
            pltpu.VMEM((slots, rows, LANES), F32),
            pltpu.VMEM((2 * nb, 3 * LANES), F32),
            pltpu.VMEM((2 * nb, LANES, 3 * LANES), BF16),
            pltpu.VMEM((2 * nb, LANES, 3 * LANES), BF16),
            pltpu.SemaphoreType.DMA((slots,)),
            pltpu.SemaphoreType.DMA((slots,)),
            pltpu.SemaphoreType.DMA((nr,)),
            pltpu.SemaphoreType.DMA((nr,)),
            pltpu.SemaphoreType.DMA((nb * nr,)),
            pltpu.SemaphoreType.DMA((nb * nr,)),
            pltpu.SemaphoreType.DMA((len(operands),)),
        ],
        compiler_params=pltpu.CompilerParams(
            collective_id=0, has_side_effects=True, vmem_limit_bytes=62 * 1024 * 1024
        ),
    )(*operands)
    return both[0], both[1] / autocorrelation.shape[2]


def solution(mesh):
    return jax.shard_map(
        body,
        mesh=mesh,
        in_specs=(
            P("rate", ("parts", "bank", "tm")),
            P(("parts", "bank", "tm")),
            P(("parts", "bank", "tm")),
            P("rate", None),
            P("rate", None),
            P("bank", "rate", None, None),
            P("bank"),
            P("bank", "rate", None, None, None),
            P(),
        ),
        out_specs=(
            P(None, "rate", ("parts", "bank", "tm")),
            P(None, "rate", ("parts", "bank", "tm")),
        ),
        check_vma=False,
    )
```
